128 devices in a mesh: dev: 128 (over x, z, y, core).
Axes of the slice: x: 4, y: 4, z: 4, core: 2. Of those that a mesh axis runs over, the one named last changes fastest.
Arguments:
- coefficients: bfloat16 [512, 4, 128, 128], P('dev'), may hold values from -6 to 6
- send_tile: int32 [128, 128], P('dev'), may hold values from 0 to 3
- slot_external: int32 [128, 128], P('dev'), may hold values from 0 to 7
- slot_pairs: int32 [128, 128, 3], P('dev'), may hold values from 0 to 63
- factor_alpha: bfloat16 [64, 128, 128], replicated, may hold values from -0.5 to 0.5
- factor_beta: bfloat16 [64, 128, 128], replicated, may hold values from -0.5 to 0.5
- denominators: float32 [1024, 4, 128, 128], P('dev'), may hold values from 4 to 32
Outputs:
- amplitudes: bfloat16 [1024, 4, 128, 128], P('dev')
- dressing: float32 [512, 4, 128, 128], P('dev')
- gram: float32 [4, 4], replicated
The draws below stay inside these ranges and needn't reach their ends.
All inputs are finite; a program needn't handle non-finite values.
Results may differ from the reference program's by a relative error of at most 0.004.
The reference program's roundings to bfloat16 on the way count: a program that leaves them out, or rounds other values in their place, can miss the bound.
Values may be sent and summed in bfloat16 or wider, within the bound.
A program may use at most 128 MiB of HBM per device.

```python
import math
import jax
import jax.numpy as jnp
import numpy as np
from jax import lax

S = 4
A = 128
V_DEV = 4
E_DEV = 8
J = 3
P_SIZE = 64
VT = 512
ET = 1024
N_DEV = 128


def touch_ends(entries, stream_key, low, high):
    shape = entries.shape
    spot = [jax.random.randint(jax.random.fold_in(stream_key, axis), (), 0, shape[axis]) for axis in range(len(shape))]
    entries = entries.at[tuple(spot)].set(low)
    longest = shape.index(max(shape))
    spot[longest] = (spot[longest] + 1) % shape[longest]
    return entries.at[tuple(spot)].set(high)


def shard_levels(own_key, dims, pieces, least, top_value):
    factor_of, own = 1.0, jax.random.fold_in(own_key, 6)
    for axis_at, blocks in pieces:
        heights = jnp.exp(jax.random.uniform(jax.random.fold_in(own, axis_at), (blocks,), jnp.float32, least / len(pieces), top_value / len(pieces)))
        factor_of = factor_of * jnp.repeat(heights, dims[axis_at] // blocks).reshape([-1 if axis == axis_at else 1 for axis in range(len(dims))])
    return factor_of


def cumulative_ranks(number_of, slope):
    portions = [(1 << 20) // math.isqrt(grade ** slope) + 1 for grade in range(1, number_of + 1)]
    spread = 1 + sum(portions) // (1 << 30)
    return np.cumsum(np.array([max(1, weight // spread) for weight in portions]))


def ranked(rng, extent, number_of, skew):
    table = cumulative_ranks(number_of, skew)
    lot = jax.random.randint(jax.random.fold_in(rng, 1), extent, 0, int(table[number_of - 1]))
    rank = jnp.searchsorted(jnp.asarray(table, jnp.int32), lot, side="right")
    return jax.random.permutation(jax.random.fold_in(rng, 2), number_of)[rank].astype(jnp.int32)


def bell_draw(rng, dims, spread, limit, cuts=(), kind=jnp.bfloat16):
    result = jax.random.normal(rng, dims, jnp.float32) * spread
    if len(cuts) > 0:
        result = shard_levels(rng, dims, cuts, -0.22, 0.18) * result
    return jnp.clip(result, min=-limit, max=limit).astype(kind)


def setup_inputs(seed: int = 0) -> dict:
    streams_of = jax.random.split(jax.random.key(seed), 8)
    return {
        "coefficients": bell_draw(streams_of[0], (VT, S, A, A), 1.0, 6.0, ((0, 128),)),
        "send_tile": touch_ends(jax.random.randint(streams_of[1], (N_DEV, N_DEV), 0, V_DEV), jax.random.fold_in(streams_of[1], 1), 0, V_DEV - 1).astype(jnp.int32),
        "slot_external": touch_ends(ranked(streams_of[2], (N_DEV, N_DEV), E_DEV, 2), jax.random.fold_in(streams_of[2], 3), 0, E_DEV - 1).astype(jnp.int32),
        "slot_pairs": touch_ends(jax.random.randint(streams_of[3], (N_DEV, N_DEV, J), 0, P_SIZE), jax.random.fold_in(streams_of[3], 1), 0, P_SIZE - 1).astype(jnp.int32),
        "factor_alpha": bell_draw(streams_of[4], (P_SIZE, A, A), A ** -0.5, 0.5),
        "factor_beta": bell_draw(streams_of[5], (P_SIZE, A, A), A ** -0.5, 0.5),
        "denominators": jnp.clip(jnp.exp(math.log(32.0) - 2.0794415 * jax.random.uniform(streams_of[6], (ET, S, A, A), jnp.float32) ** shard_levels(streams_of[6], (ET, S, A, A), ((0, 128),), -0.2, 0.2)), 4.0, 32.0),
    }


def pair_forward(slot_tiles, pair_rows, factor_alpha, factor_beta):
    left_factor = factor_alpha[pair_rows].astype(jnp.float32)
    right_factor = factor_beta[pair_rows].astype(jnp.float32)
    half_product = jnp.einsum('njab,nsac->njsbc', left_factor, slot_tiles.astype(jnp.float32), precision=lax.Precision.HIGHEST).astype(jnp.bfloat16)
    half_product = lax.optimization_barrier(half_product).astype(jnp.float32)
    return jnp.einsum('njsbc,njcd->nsbd', half_product, right_factor, precision=lax.Precision.HIGHEST).astype(jnp.bfloat16)


def pair_adjoint(amplitude_slots, pair_rows, factor_alpha, factor_beta):
    left_factor = factor_alpha[pair_rows].astype(jnp.float32)
    right_factor = factor_beta[pair_rows].astype(jnp.float32)
    half_product = jnp.einsum('njab,nsbd->njsad', left_factor, amplitude_slots.astype(jnp.float32), precision=lax.Precision.HIGHEST).astype(jnp.bfloat16)
    half_product = lax.optimization_barrier(half_product).astype(jnp.float32)
    return jnp.einsum('njsad,njcd->nsac', half_product, right_factor, precision=lax.Precision.HIGHEST).astype(jnp.bfloat16)


def reference(coefficients, send_tile, slot_external, slot_pairs, factor_alpha, factor_beta, denominators):
    by_owner = coefficients.reshape(N_DEV, V_DEV, S, A, A)
    owners = jnp.arange(N_DEV, dtype=jnp.int32)
    external_range = jnp.arange(E_DEV, dtype=jnp.int32)
    tile_range = jnp.arange(V_DEV, dtype=jnp.int32)

    def forward(receiver):
        slot_tiles = by_owner[owners, send_tile[:, receiver]]
        coupling = pair_forward(slot_tiles, slot_pairs[receiver], factor_alpha, factor_beta)
        onehot = (slot_external[receiver][:, None] == external_range[None, :]).astype(jnp.float32)
        return jnp.einsum('ne,nsbd->esbd', onehot, coupling.astype(jnp.float32), precision=lax.Precision.HIGHEST)

    sigma_sum = lax.map(forward, owners).reshape(E_DEV * N_DEV, S, A, A)
    amplitudes = (sigma_sum / denominators).astype(jnp.bfloat16)
    gram = jnp.einsum('esbd,etbd->st', sigma_sum, amplitudes.astype(jnp.float32), precision=lax.Precision.HIGHEST) / (E_DEV * N_DEV * A * A)
    by_device = amplitudes.reshape(N_DEV, E_DEV, S, A, A)

    def backward(dressing_sum, receiver):
        amplitude_slots = by_device[receiver][slot_external[receiver]]
        partial_value = pair_adjoint(amplitude_slots, slot_pairs[receiver], factor_alpha, factor_beta)
        onehot = (send_tile[:, receiver][:, None] == tile_range[None, :]).astype(jnp.float32)
        return dressing_sum + onehot[:, :, None, None, None] * partial_value.astype(jnp.float32)[:, None], None

    dressing_sum, _ = lax.scan(backward, jnp.zeros((N_DEV, V_DEV, S, A, A), jnp.float32), owners)
    return amplitudes, dressing_sum.reshape(V_DEV * N_DEV, S, A, A), gram
```

```python
import functools

import jax
import jax.numpy as jnp
from jax import lax
from jax.experimental import pallas as pl
from jax.experimental.pallas import tpu as pltpu
from jax.sharding import PartitionSpec as P

BF = jnp.bfloat16
F = jnp.float32
MESH = pl.DeviceIdType.MESH
A = 128
C = 2
Q = 2
U = 8
FWD, BWD = 0, 1024
LAST_F, SOME_F = 2048, 2112
LAST_B, SOME_B = 2176, 2240
TABLE = 2304


def place():
    me = lax.axis_index("dev")
    return lax.div(me, 32), lax.rem(lax.div(me, 8), 4), lax.rem(lax.div(me, 2), 4), lax.rem(me, 2)


def device(x, z, y, c):
    return ((x * 4 + z) * 4 + y) * 2 + c


def up(i, d):
    return lax.rem(i + d, 4)


class remote:
    def __init__(self, src, dst, send, recv, to):
        self.what = (src, dst, send, recv, to)

    def copy(self):
        src, dst, send, recv, to = self.what
        return pltpu.make_async_remote_copy(
            src_ref=src, dst_ref=dst, send_sem=send, recv_sem=recv, device_id=(to,), device_id_type=MESH
        )

    def start(self):
        self.copy().start()

    def wait_send(self):
        self.copy().wait_send()

    def wait_recv(self):
        self.copy().wait_recv()


def greet(peers):
    barrier = pltpu.get_barrier_semaphore()
    for p in peers:
        pl.semaphore_signal(barrier, inc=1, device_id=(p,), device_id_type=MESH)
    pl.semaphore_wait(barrier, len(peers))


def table_kernel(own, plane_out, ring_out, plane, ring, send_p, recv_p, send_r, recv_r):
    x, z, y, c = place()
    in_plane = [(up(x, i // 4), up(z, i % 4), y, c) for i in range(1, 16)]
    in_ring = [(x, z, up(y, i // 2), lax.rem(c + i, 2)) for i in range(1, 8)]
    greet([device(*p) for p in in_plane + in_ring])
    copies = []
    for i, p in enumerate(in_plane):
        copies.append(remote(own, plane.at[i], send_p.at[i], recv_p.at[i], device(*p)))
    for i, p in enumerate(in_ring):
        copies.append(remote(own, ring.at[i], send_r.at[i], recv_r.at[i], device(*p)))
    for copy in copies:
        copy.start()
    plane_out[x * 4 + z] = own[...]
    ring_out[y * 2 + c] = own[...]
    for copy in copies:
        copy.wait_send()
        copy.wait_recv()
    for i in range(1, 16):
        plane_out[up(x, 4 - i // 4) * 4 + up(z, 4 - i % 4)] = plane[i - 1]
    for i in range(1, 8):
        ring_out[up(y, 4 - i // 2) * 2 + lax.rem(c + i, 2)] = ring[i - 1]


def exchange_tables(own):
    return pl.pallas_call(
        table_kernel,
        out_shape=(
            jax.ShapeDtypeStruct((16, 8, 128), jnp.int32),
            jax.ShapeDtypeStruct((8, 8, 128), jnp.int32),
        ),
        in_specs=[pl.BlockSpec(memory_space=pltpu.VMEM)],
        out_specs=[pl.BlockSpec(memory_space=pltpu.VMEM)] * 2,
        scratch_shapes=[
            pltpu.VMEM((15, 8, 128), jnp.int32),
            pltpu.VMEM((7, 8, 128), jnp.int32),
            pltpu.SemaphoreType.DMA((15,)),
            pltpu.SemaphoreType.DMA((15,)),
            pltpu.SemaphoreType.DMA((7,)),
            pltpu.SemaphoreType.DMA((7,)),
        ],
        compiler_params=pltpu.CompilerParams(collective_id=0, has_side_effects=True),
    )(own)


def dot(a, b):
    return jnp.dot(a, b, preferred_element_type=F)


def connection(tile, left, right):
    wide = jnp.concatenate([tile[s] for s in range(C)], axis=1)
    half = dot(jnp.concatenate(left, axis=0), wide).astype(BF)
    rows = [
        jnp.concatenate(
            [half[j * A : (j + 1) * A, s * A : (s + 1) * A] for j in range(len(left))], axis=1
        )
        for s in range(C)
    ]
    return dot(jnp.concatenate(rows, axis=0), jnp.concatenate(right, axis=0))


def main_kernel(
    table, coef, left_f, right_f, left_b, right_b, den_hbm,
    amps, dress, gram,
    G0, G1, LF, RF, LB, RB, den, S, Out, RecvC, RecvY, sigma, Amp0, Amp1, RecvZ, RecvX, RecvZ2, RecvX2,
    own_gram, peer_gram, loc, ag_s, ag_r, c_s, c_r, y_s, y_r, ga_s, ga_r, z_s, z_r, x_s, x_r,
    z2_s, z2_r, x2_s, x2_r, gr_s, gr_r,
):
    x, z, y, c = place()
    G, Amp = (G0, G1), (Amp0, Amp1)
    other = 1 - c
    core = device(x, z, y, other)
    xs = [device(up(x, d), z, y, c) for d in range(4)]
    zs = [device(x, up(z, d), y, c) for d in range(4)]
    ys = [device(x, z, up(y, d), c) for d in range(4)]

    def own_tiles(q):
        return pltpu.make_async_copy(
            coef.at[:, pl.ds(q * C, C)], G[q].at[x, z], loc.at[q]
        )

    loads = [
        pltpu.make_async_copy(src, dst, loc.at[2 + i])
        for i, (src, dst) in enumerate(
            [(left_f, LF), (right_f, RF), (left_b, LB), (right_b, RB), (den_hbm, den)]
        )
    ]
    for q in range(Q):
        own_tiles(q).start()
    for load in loads:
        load.start()
    greet(xs[1:] + zs[1:] + ys[1:] + [core])

    def gather_copies(q, h):
        lo = 2 * h
        one = pl.ds(lo, 2)
        near, far = (xs, zs) if h == 0 else (zs, xs)

        def at(d, e):
            dx, dz = (d, e) if h == 0 else (e, d)
            ix = pl.ds(0, 4) if dx is None else up(x, dx)
            iz = pl.ds(0, 4) if dz is None else up(z, dz)
            return ix, iz

        def sems(k):
            return ag_s.at[q, h, k], ag_r.at[q, h, k]

        def block(d, e, tiles):
            ix, iz = at(d, e)
            return G[q].at[ix, iz, tiles]

        src = coef.at[one, pl.ds(q * C, C)]
        first, second = pl.ds(lo, 1), pl.ds(lo + 1, 1)
        sends = [
            remote(src, block(0, 0, one), *sems(0), near[1]),
            remote(src, block(0, 0, one), *sems(1), near[3]),
            remote(block(3, 0, first), block(3, 0, first), *sems(2), near[1]),
            remote(block(1, 0, second), block(1, 0, second), *sems(3), near[3]),
            remote(block(None, 0, one), block(None, 0, one), *sems(4), far[1]),
            remote(block(None, 0, one), block(None, 0, one), *sems(5), far[3]),
            remote(block(None, 3, first), block(None, 3, first), *sems(6), far[1]),
            remote(block(None, 1, second), block(None, 1, second), *sems(7), far[3]),
        ]
        landed = [
            block(3, 0, one), block(1, 0, one), block(2, 0, first), block(2, 0, second),
            block(None, 3, one), block(None, 1, one), block(None, 2, first), block(None, 2, second),
        ]
        recvs = [remote(b, b, *sems(k), near[1]) for k, b in enumerate(landed)]
        return sends, recvs

    def gather_step(q, step):
        for h in range(2):
            sends, recvs = gather_copies(q, h)
            for k in (2 * step, 2 * step + 1):
                if step in (1, 3):
                    recvs[k - 2].wait_recv()
                if step == 2:
                    recvs[k - 2].wait_recv()
            if step == 2 and h == 0:
                own_tiles(q).wait()
            if step == 4:
                recvs[6].wait_recv()
                recvs[7].wait_recv()
            else:
                for k in (2 * step, 2 * step + 1):
                    sends[k].start()

    def gather_done(q):
        for h in range(2):
            for copy in gather_copies(q, h)[0]:
                copy.wait_send()

    def sums(count, fetch, base):
        def step(i, run):
            terms = []
            for u in range(U):
                k = base + (i * U + u) * 8
                tile, keep, lefts, rights = fetch(k)
                terms.append((keep, connection(tile, lefts, rights)))
            for u, (keep, term) in enumerate(terms):
                run = run * keep + term
                S[i * U + u] = run
            return run

        zero = jnp.zeros((C * A, A), F)
        if count == U:
            step(0, zero)
        else:
            lax.fori_loop(0, count // U, step, zero)

    def picked(last, some, i):
        return S[table[last + i]] * table[some + i].astype(F)

    def fetch_f(q):
        def fetch(k):
            tile = G[q][table[k], table[k + 1], table[k + 2]]
            pairs = [table[k + 3 + j] for j in range(3)]
            return tile, table[k + 6].astype(F), [LF[p] for p in pairs], [RF[p] for p in pairs]

        return fetch

    def core_copy(q, t):
        row = up(y, 1 + t)
        return remote(Out.at[q, pl.ds((row * 2 + other) * 8, 8)], RecvC.at[q, row], c_s.at[q, t], c_r.at[q, t], core)

    def core_recv(q, t):
        row = up(y, 1 + t)
        return remote(RecvC.at[q, row], RecvC.at[q, row], c_s.at[q, t], c_r.at[q, t], core)

    def y_copy(q, t):
        row = up(y, 1 + t)
        return remote(
            Out.at[q, pl.ds((row * 2 + c) * 8, 8)], RecvY.at[q, t], y_s.at[q, t], y_r.at[q, t], device(x, z, row, c)
        )

    def y_recv(q, t):
        return remote(RecvY.at[q, t], RecvY.at[q, t], y_s.at[q, t], y_r.at[q, t], core)

    def forward_other(q, t):
        row = up(y, 1 + t)
        target = row * 2 + other
        sums(16, fetch_f(q), FWD + target * 128)
        for e in range(8):
            Out[q, target * 8 + e] = picked(LAST_F, SOME_F, target * 8 + e).astype(BF).reshape(C, A, A)
        core_copy(q, t).start()

    def forward_same(q, t, send):
        row = up(y, 1 + t)
        target = row * 2 + c
        sums(16, fetch_f(q), FWD + target * 128)
        core_recv(q, t).wait_recv()
        for e in range(8):
            total = picked(LAST_F, SOME_F, target * 8 + e).reshape(C, A, A) + RecvC[q, row, e].astype(F)
            if send:
                Out[q, target * 8 + e] = total.astype(BF)
            else:
                sigma[q, e] = total
        if send:
            y_copy(q, t).start()

    def loop(n, body):
        def run(t, carry):
            body(t)
            return carry

        lax.fori_loop(0, n, run, 0)

    def finish_sigma(q):
        for t in range(3):
            y_recv(q, t).wait_recv()

        def one(e):
            total = sigma[q, e] + RecvY[q, 0, e].astype(F) + RecvY[q, 1, e].astype(F) + RecvY[q, 2, e].astype(F)
            sigma[q, e] = total
            amp = (total / den[e, pl.ds(q * C, C)]).astype(BF)
            Amp[q][y, c, e] = amp
            amps[e, pl.ds(q * C, C)] = amp

        loop(8, one)

    def amp_copies(q):
        def sems(k):
            return ga_s.at[q, k], ga_r.at[q, k]

        def block(d, e):
            return Amp[q].at[up(y, d), c, e]

        full, first, second = pl.ds(0, 8), pl.ds(0, 4), pl.ds(4, 4)

        def theirs(d):
            return Amp[q].at[up(y, d), other]

        sends = [
            remote(block(0, full), block(0, full), *sems(0), ys[1]),
            remote(block(0, full), block(0, full), *sems(1), ys[3]),
            remote(block(3, first), block(3, first), *sems(2), ys[1]),
            remote(block(1, second), block(1, second), *sems(3), ys[3]),
        ] + [remote(Amp[q].at[up(y, d), c], Amp[q].at[up(y, d), c], *sems(4 + d), core) for d in range(4)]
        landed = [block(3, full), block(1, full), block(2, first), block(2, second)]
        landed += [theirs(d) for d in range(4)]
        recvs = [remote(b, b, *sems(k), core) for k, b in enumerate(landed)]
        return sends, recvs

    def amp_step(q, step):
        sends, recvs = amp_copies(q)
        if step == 0:
            for k in (0, 1, 4):
                sends[k].start()
        if step == 1:
            recvs[0].wait_recv()
            sends[2].start()
            sends[7].start()
            recvs[1].wait_recv()
            sends[3].start()
            sends[5].start()
        if step == 2:
            recvs[2].wait_recv()
            recvs[3].wait_recv()
            sends[6].start()
        if step == 3:
            for k in range(4, 8):
                recvs[k].wait_recv()

    def amp_done(q):
        for copy in amp_copies(q)[0]:
            copy.wait_send()

    def fetch_b(q):
        def fetch(k):
            tile = Amp[q][table[k], table[k + 1], table[k + 2]]
            pairs = [table[k + 3 + j] for j in range(3)]
            return tile, table[k + 6].astype(F), [LB[p] for p in pairs], [RB[p] for p in pairs]

        return fetch

    def z_copy(q, a, b):
        iz, ix = up(z, 1 + a), up(x, 1 + b)
        return remote(
            Out.at[q, pl.ds((ix * 4 + iz) * 4, 2)], RecvZ.at[q, a, ix], z_s.at[q, a], z_r.at[q, a],
            device(x, iz, y, c),
        )

    def x_copy(q, a, b):
        iz, ix = up(z, 1 + a), up(x, 1 + b)
        return remote(
            Out.at[q, pl.ds((ix * 4 + iz) * 4 + 2, 2)], RecvX.at[q, b, iz], x_s.at[q, b], x_r.at[q, b],
            device(ix, z, y, c),
        )

    def backward(q, t):
        a, b = lax.div(t, 4), lax.rem(t, 4)
        target = up(x, 1 + b) * 4 + up(z, 1 + a)
        sums(8, fetch_b(q), BWD + target * 64)
        for v in range(4):
            Out[q, target * 4 + v] = picked(LAST_B, SOME_B, target * 4 + v).astype(BF).reshape(C, A, A)

        @pl.when(a < 3)
        def _():
            z_copy(q, a, b).start()

        @pl.when(b < 3)
        def _():
            x_copy(q, a, b).start()

    def z2_copy(q, i):
        ix = up(x, 1 + i)
        return remote(
            Out.at[q, pl.ds((ix * 4 + z) * 4, 2)], RecvZ2.at[q, i], z2_s.at[q, i], z2_r.at[q, i],
            device(ix, z, y, c),
        )

    def x2_copy(q, i):
        iz = up(z, 1 + i)
        return remote(
            Out.at[q, pl.ds((x * 4 + iz) * 4 + 2, 2)], RecvX2.at[q, i], x2_s.at[q, i], x2_r.at[q, i],
            device(x, iz, y, c),
        )

    def whole(buffer, send, recv):
        return remote(buffer, buffer, send, recv, core)

    def second_stage(q):
        for a in range(3):
            whole(RecvZ.at[q, a], z_s.at[q, a], z_r.at[q, a]).wait_recv()
            whole(RecvX.at[q, a], x_s.at[q, a], x_r.at[q, a]).wait_recv()

        def total(at, recv, i, v):
            return Out[q, at + v].astype(F) + recv[q, 0, i, v].astype(F) + recv[q, 1, i, v].astype(F) + recv[q, 2, i, v].astype(F)

        def one(i):
            ix, iz = up(x, 1 + i), up(z, 1 + i)
            at_z, at_x = (ix * 4 + z) * 4, (x * 4 + iz) * 4 + 2
            for v in range(2):
                Out[q, at_z + v] = total(at_z, RecvZ, ix, v).astype(BF)
            z2_copy(q, i).start()
            for v in range(2):
                Out[q, at_x + v] = total(at_x, RecvX, iz, v).astype(BF)
            x2_copy(q, i).start()

        loop(3, one)
        at = (x * 4 + z) * 4
        for v in range(2):
            dress[v, pl.ds(q * C, C)] = total(at, RecvZ, x, v)
            dress[2 + v, pl.ds(q * C, C)] = total(at + 2, RecvX, z, v)

    def last_stage(q):
        for i in range(3):
            whole(RecvZ2.at[q, i], z2_s.at[q, i], z2_r.at[q, i]).wait_recv()
            whole(RecvX2.at[q, i], x2_s.at[q, i], x2_r.at[q, i]).wait_recv()
        for v in range(2):
            for at, recv in ((v, RecvZ2), (2 + v, RecvX2)):
                dress[at, pl.ds(q * C, C)] = dress[at, pl.ds(q * C, C)] + (
                    recv[q, 0, v].astype(F) + recv[q, 1, v].astype(F) + recv[q, 2, v].astype(F)
                )

    def local_gram():
        def one(e, total):
            sig = [sigma[s // C, e, s % C] for s in range(4)]
            amp = [amps[e, s].astype(F) for s in range(4)]
            return tuple(
                total[s * 4 + t] + (sig[s] * amp[t]).reshape(16, 8, A).sum(axis=0)
                for s in range(4)
                for t in range(4)
            )

        sums_ = lax.fori_loop(0, 8, one, tuple(jnp.zeros((8, A), F) for _ in range(16)))
        row = lax.broadcasted_iota(jnp.int32, (8, A), 0)
        col = lax.broadcasted_iota(jnp.int32, (8, A), 1)
        out = jnp.zeros((8, A), F)
        for s in range(4):
            for t in range(4):
                value = jnp.sum(sums_[s * 4 + t]) / (1024.0 * A * A)
                out = out + jnp.where((row == s) & (col == t), value, 0.0)
        own_gram[0] = out

    gram_axes = ((0, 3, xs), (3, 3, zs), (6, 3, ys), (9, 1, [None, core]))

    def gram_send(k):
        first, n, devs = gram_axes[k]
        for i in range(n):
            remote(own_gram.at[k], peer_gram.at[first + i], gr_s.at[first + i], gr_r.at[first + i], devs[1 + i]).start()

    def gram_take(k):
        first, n, _ = gram_axes[k]
        out = own_gram[k]
        for i in range(n):
            whole(peer_gram.at[first + i], gr_s.at[first + i], gr_r.at[first + i]).wait_recv()
            out = out + peer_gram[first + i]
        own_gram[k + 1] = out

    for step in range(4):
        gather_step(0, step)
    for load in loads:
        load.wait()
    gather_step(0, 4)
    gather_step(1, 0)
    loop(1, lambda t: forward_other(0, t))
    gather_step(1, 1)
    loop(2, lambda t: forward_other(0, t + 1))
    gather_step(1, 2)
    loop(1, lambda t: forward_other(0, t + 3))
    loop(2, lambda t: forward_same(0, t, True))
    gather_step(1, 3)
    loop(1, lambda t: forward_same(0, t + 2, True))
    loop(1, lambda t: forward_same(0, t + 3, False))
    gather_step(1, 4)
    loop(4, lambda t: forward_other(1, t))
    finish_sigma(0)
    amp_step(0, 0)
    loop(2, lambda t: forward_same(1, t, True))
    amp_step(0, 1)
    loop(1, lambda t: forward_same(1, t + 2, True))
    amp_step(0, 2)
    loop(1, lambda t: forward_same(1, t + 3, False))
    amp_step(0, 3)
    for t in range(4):
        core_copy(0, t).wait_send()
    for t in range(3):
        y_copy(0, t).wait_send()
    loop(4, lambda t: backward(0, t))
    finish_sigma(1)
    amp_step(1, 0)
    local_gram()
    gram_send(0)
    loop(4, lambda t: backward(0, t + 4))
    amp_step(1, 1)
    gram_take(0)
    gram_send(1)
    loop(4, lambda t: backward(0, t + 8))
    amp_step(1, 2)
    gram_take(1)
    gram_send(2)
    loop(4, lambda t: backward(0, t + 12))
    amp_step(1, 3)
    gram_take(2)
    gram_send(3)
    for t in range(4):
        core_copy(1, t).wait_send()
    for t in range(3):
        y_copy(1, t).wait_send()
    loop(8, lambda t: backward(1, t))
    for a in range(3):
        whole(RecvZ.at[0, a], z_s.at[0, a], z_r.at[0, a]).wait_send()
        whole(RecvX.at[0, a], x_s.at[0, a], x_r.at[0, a]).wait_send()
    second_stage(0)
    loop(8, lambda t: backward(1, t + 8))
    last_stage(0)
    gram_take(3)
    gram[...] = own_gram[4]
    for a in range(3):
        whole(RecvZ.at[1, a], z_s.at[1, a], z_r.at[1, a]).wait_send()
        whole(RecvX.at[1, a], x_s.at[1, a], x_r.at[1, a]).wait_send()
    second_stage(1)
    last_stage(1)
    for q in range(Q):
        gather_done(q)
        amp_done(q)
        for i in range(3):
            z2_copy(q, i).wait_send()
            x2_copy(q, i).wait_send()
    for k in range(10):
        whole(peer_gram.at[k], gr_s.at[k], gr_r.at[k]).wait_send()


def run_main(table, coefficients, left_f, right_f, left_b, right_b, denominators):
    dma = pltpu.SemaphoreType.DMA
    tiles = lambda *n: pltpu.VMEM((*n, C, A, A), BF)
    factor = pltpu.VMEM((64, A, A), BF)
    return pl.pallas_call(
        main_kernel,
        out_shape=(
            jax.ShapeDtypeStruct((8, 4, A, A), BF),
            jax.ShapeDtypeStruct((4, 4, A, A), F),
            jax.ShapeDtypeStruct((8, A), F),
        ),
        in_specs=[pl.BlockSpec(memory_space=pltpu.SMEM)] + [pl.BlockSpec(memory_space=pl.ANY)] * 6,
        out_specs=[pl.BlockSpec(memory_space=pltpu.VMEM)] * 3,
        scratch_shapes=[
            tiles(4, 4, 4), tiles(4, 4, 4),
            factor, factor, factor, factor,
            pltpu.VMEM((8, 4, A, A), F),
            pltpu.VMEM((16, C * A, A), F),
            tiles(Q, 64),
            tiles(Q, 4, 8),
            tiles(Q, 3, 8),
            pltpu.VMEM((Q, 8, C, A, A), F),
            tiles(4, 2, 8), tiles(4, 2, 8),
            tiles(Q, 3, 4, 2),
            tiles(Q, 3, 4, 2),
            tiles(Q, 3, 2),
            tiles(Q, 3, 2),
            pltpu.VMEM((5, 8, A), F),
            pltpu.VMEM((10, 8, A), F),
            dma((7,)),
            dma((Q, 2, 8)), dma((Q, 2, 8)),
            dma((Q, 4)), dma((Q, 4)),
            dma((Q, 3)), dma((Q, 3)),
            dma((Q, 8)), dma((Q, 8)),
            dma((Q, 3)), dma((Q, 3)), dma((Q, 3)), dma((Q, 3)),
            dma((Q, 3)), dma((Q, 3)), dma((Q, 3)), dma((Q, 3)),
            dma((10,)), dma((10,)),
        ],
        compiler_params=pltpu.CompilerParams(
            collective_id=1, has_side_effects=True, vmem_limit_bytes=60 * 2**20
        ),
    )(table, coefficients, left_f, right_f, left_b, right_b, denominators)


def in_order(key, fields, targets):
    k = key.shape[1]
    at = jnp.arange(k, dtype=jnp.int32)
    before = (key[:, :, None] > key[:, None, :]) | (
        (key[:, :, None] == key[:, None, :]) & (at[:, None] > at[None, :])
    )
    rank = jnp.sum(before.astype(jnp.int32), axis=2)
    onehot = (rank[:, None, :] == at[None, :, None]).astype(jnp.int32)
    full = jnp.concatenate([fields, key[:, :, None]], axis=2)
    ordered = jnp.sum(onehot[:, :, :, None] * full[:, None, :, :], axis=2)
    key = ordered[:, :, 6]
    keep = (key == jnp.concatenate([jnp.full_like(key[:, :1], -1), key[:, :-1]], axis=1)).astype(jnp.int32)
    ordered = jnp.concatenate([ordered[:, :, :6], keep[:, :, None], keep[:, :, None]], axis=2)
    values = jnp.arange(targets, dtype=jnp.int32)
    last = jnp.sum((key[:, :, None] <= values).astype(jnp.int32), axis=1) - 1
    some = jnp.sum((key[:, :, None] == values).astype(jnp.int32), axis=1) > 0
    return ordered, jnp.maximum(last, 0), some.astype(jnp.int32)


def per_device(coefficients, send_tile, slot_external, slot_pairs, factor_alpha, factor_beta, denominators):
    me = lax.axis_index("dev")
    ring, spot = me // 8, me % 8
    own = jnp.concatenate(
        [send_tile, slot_external, slot_pairs[0].T, jnp.zeros((3, 128), jnp.int32)], axis=0
    )
    planes, rings = exchange_tables(own)
    tile = lax.dynamic_index_in_dim(planes[:, 0].reshape(16, 16, 8), ring, 1, False)
    mine = lax.dynamic_index_in_dim(rings.reshape(8, 8, 16, 8), spot, 3, False)
    external = mine[:, 1]
    pairs = mine[:, 2:5].transpose(0, 2, 1)
    owner = jnp.arange(16, dtype=jnp.int32)
    receiver = jnp.arange(8, dtype=jnp.int32)

    def spread(a, shape):
        return jnp.broadcast_to(a, shape)[:, :, None]

    fields_f = jnp.concatenate(
        [spread(owner // 4, (8, 16)), spread(owner % 4, (8, 16)), tile.T[:, :, None], pairs], axis=2
    )
    fields_b = jnp.concatenate(
        [
            spread(receiver // 2, (16, 8)),
            spread(receiver % 2, (16, 8)),
            external.T[:, :, None],
            pairs.transpose(1, 0, 2),
        ],
        axis=2,
    )
    parts = [*in_order(external, fields_f, 8), *in_order(tile, fields_b, 4)]
    table = jnp.concatenate([parts[i].reshape(-1) for i in (0, 3, 1, 2, 4, 5)])
    turn = lambda f: jnp.swapaxes(f, 1, 2)
    amplitudes, dressing, gram = run_main(
        table, coefficients, turn(factor_alpha), factor_beta, factor_alpha, turn(factor_beta), denominators
    )
    return amplitudes, dressing, gram[:4, :4]


def solution(mesh):
    return jax.shard_map(
        per_device,
        mesh=mesh,
        in_specs=(
            P("dev", None, None, None),
            P("dev", None),
            P("dev", None),
            P("dev", None, None),
            P(),
            P(),
            P("dev", None, None, None),
        ),
        out_specs=(P("dev", None, None, None), P("dev", None, None, None), P()),
        check_vma=False,
    )
```

```python
import functools

import jax
import jax.numpy as jnp
from jax import lax
from jax.experimental import pallas as pl
from jax.experimental.pallas import tpu as pltpu
from jax.sharding import PartitionSpec as P

BF = jnp.bfloat16
F = jnp.float32
MESH = pl.DeviceIdType.MESH
A = 128
C = 2
Q = 2
U = 8
FWD, BWD = (0, 1024), (2048, 3072)
LAST_F, SOME_F = (4096, 4160), (4224, 4288)
LAST_B, SOME_B = (4352, 4416), (4480, 4544)


def place():
    me = lax.axis_index("dev")
    return lax.div(me, 32), lax.rem(lax.div(me, 8), 4), lax.rem(lax.div(me, 2), 4), lax.rem(me, 2)


def device(x, z, y, c):
    return ((x * 4 + z) * 4 + y) * 2 + c


def up(i, d):
    return lax.rem(i + d, 4)


def step_of(t):
    if isinstance(t, int):
        return (2, 1, 3, 0)[t]
    return jnp.where(t == 0, 2, jnp.where(t == 3, 0, 2 * t - 1))


class remote:
    def __init__(self, src, dst, send, recv, to):
        self.what = (src, dst, send, recv, to)

    def copy(self):
        src, dst, send, recv, to = self.what
        return pltpu.make_async_remote_copy(
            src_ref=src, dst_ref=dst, send_sem=send, recv_sem=recv, device_id=(to,), device_id_type=MESH
        )

    def start(self):
        self.copy().start()

    def wait_send(self):
        self.copy().wait_send()

    def wait_recv(self):
        self.copy().wait_recv()


def greet(peers):
    barrier = pltpu.get_barrier_semaphore()
    for p in peers:
        pl.semaphore_signal(barrier, inc=1, device_id=(p,), device_id_type=MESH)
    pl.semaphore_wait(barrier, len(peers))


STEPS = [
    (dx, dz, dy, dc)
    for dx in range(4)
    for dz in range(4)
    for dy in range(4)
    for dc in range(2)
    if (dy, dc) == (0, 0) or (dx, dz) == (0, 0) or (dx, dc) == (0, 0) or (dz, dy) == (0, 0)
]


def table_kernel(own, planes, rings, rows, send, recv):
    x, z, y, c = place()

    def to(d):
        return up(x, d[0]), up(z, d[1]), up(y, d[2]), lax.rem(c + d[3], 2)

    others = STEPS[1:]
    greet([device(*to(d)) for d in others])
    copies = [
        remote(own, rows.at[i], send.at[i], recv.at[i], device(*to(d))) for i, d in enumerate(others)
    ]
    for copy in copies:
        copy.start()
    for i, d in enumerate(STEPS):
        if i:
            copies[i - 1].wait_recv()
        row = own[...] if i == 0 else rows[i - 1]
        fx, fz, fy, fc = to([4 - v for v in d])
        if d[2] == 0 and d[3] == 0:
            planes[0, fx * 4 + fz] = row
        if d[0] == 0 and d[1] == 0:
            rings[0, fy * 2 + fc] = row
        if d[0] == 0 and d[3] == 0:
            planes[1, fy * 4 + fz] = row
        if d[1] == 0 and d[2] == 0:
            rings[1, fx * 2 + fc] = row
    for copy in copies:
        copy.wait_send()


def exchange_tables(own):
    n = len(STEPS) - 1
    return pl.pallas_call(
        table_kernel,
        out_shape=(
            jax.ShapeDtypeStruct((2, 16, 8, 128), jnp.int32),
            jax.ShapeDtypeStruct((2, 8, 8, 128), jnp.int32),
        ),
        in_specs=[pl.BlockSpec(memory_space=pltpu.VMEM)],
        out_specs=[pl.BlockSpec(memory_space=pltpu.VMEM)] * 2,
        scratch_shapes=[
            pltpu.VMEM((n, 8, 128), jnp.int32),
            pltpu.SemaphoreType.DMA((n,)),
            pltpu.SemaphoreType.DMA((n,)),
        ],
        compiler_params=pltpu.CompilerParams(collective_id=0, has_side_effects=True),
    )(own)


def dot(a, b):
    return jnp.dot(a, b, preferred_element_type=F)


def connection(tile, left, right):
    wide = jnp.concatenate([tile[s] for s in range(C)], axis=1)
    half = dot(jnp.concatenate(left, axis=0), wide).astype(BF)
    rows = [
        jnp.concatenate(
            [half[j * A : (j + 1) * A, s * A : (s + 1) * A] for j in range(len(left))], axis=1
        )
        for s in range(C)
    ]
    return dot(jnp.concatenate(rows, axis=0), jnp.concatenate(right, axis=0))


def main_kernel(
    table, coef, alpha, beta, den_hbm,
    amps, dress, gram,
    G0, G1, LF, RF, LB, RB, den, S, Out, RecvC, RecvY, sigma, Amp0, Amp1, RecvZ, RecvX, RecvZ2, RecvX2,
    own_gram, peer_gram, loc, ag_s, ag_r, c_s, c_r, y_s, y_r, ga_s, ga_r, z_s, z_r, x_s, x_r,
    z2_s, z2_r, x2_s, x2_r, gr_s, gr_r,
):
    px, pz, py, c = place()
    G, Amp = (G0, G1), (Amp0, Amp1)
    other = 1 - c
    core = device(px, pz, py, other)

    def role(q):
        return (px, pz, py) if q == 0 else (py, pz, px)

    def at_role(q, x, z, y):
        return device(x, z, y, c) if q == 0 else device(y, z, x, c)

    def xs(q):
        x, z, y = role(q)
        return [at_role(q, up(x, d), z, y) for d in range(4)]

    def zs(q):
        x, z, y = role(q)
        return [at_role(q, x, up(z, d), y) for d in range(4)]

    def ys(q):
        x, z, y = role(q)
        return [at_role(q, x, z, up(y, d)) for d in range(4)]

    def own_tiles(q):
        x, z, _ = role(q)
        return pltpu.make_async_copy(coef.at[:, pl.ds(q * C, C)], G[q].at[x, z], loc.at[q])

    loads = [
        pltpu.make_async_copy(src, dst, loc.at[2 + i])
        for i, (src, dst) in enumerate([(alpha, LB), (beta, RF), (den_hbm, den)])
    ]
    for q in range(Q):
        own_tiles(q).start()
    for load in loads:
        load.start()
    greet(xs(0)[1:] + zs(0)[1:] + ys(0)[1:] + [core])

    def turn(src, dst):
        def step(i, carry):
            for u in range(4):
                dst[i * 4 + u] = src[i * 4 + u].T
            return carry

        lax.fori_loop(0, 16, step, 0)

    def gather_copies(q, h):
        x, z, _ = role(q)
        lo = 2 * h
        near, far = (xs(q), zs(q)) if h == 0 else (zs(q), xs(q))
        first, second, both = pl.ds(lo, 1), pl.ds(lo + 1, 1), pl.ds(lo, 2)

        def block(d, e, tiles):
            dx, dz = (d, e) if h == 0 else (e, d)
            ix = pl.ds(0, 4) if dx is None else up(x, dx)
            iz = pl.ds(0, 4) if dz is None else up(z, dz)
            return G[q].at[ix, iz, tiles]

        def sems(k):
            return ag_s.at[q, h, k], ag_r.at[q, h, k]

        sends, landed = [], []
        for stage in range(2):
            to = (near, far)[stage]

            def at(d, tiles):
                return block(d, 0, tiles) if stage == 0 else block(None, d, tiles)

            def source(tiles):
                return coef.at[tiles, pl.ds(q * C, C)] if stage == 0 else at(0, tiles)

            k = 6 * stage
            sends += [
                remote(source(first), at(0, first), *sems(k), to[1]),
                remote(source(second), at(0, second), *sems(k + 1), to[3]),
                remote(source(second), at(0, second), *sems(k + 2), to[1]),
                remote(source(first), at(0, first), *sems(k + 3), to[3]),
                remote(at(3, first), at(3, first), *sems(k + 4), to[1]),
                remote(at(1, second), at(1, second), *sems(k + 5), to[3]),
            ]
            landed += [at(3, first), at(1, second), at(3, second), at(1, first), at(2, first), at(2, second)]
        recvs = [remote(b, b, *sems(k), near[1]) for k, b in enumerate(landed)]
        return sends, recvs

    def gather_step(q, step, halves=(0, 1)):
        for h in halves:
            sends, recvs = gather_copies(q, h)
            if step in (1, 3):
                k = 6 * (step // 2)
                for i in range(2):
                    recvs[k + i].wait_recv()
                    sends[k + 4 + i].start()
            else:
                if step:
                    for k in range(2, 6):
                        recvs[3 * step - 6 + k].wait_recv()
                if step < 4:
                    for k in range(4):
                        sends[3 * step + k].start()

    def gather_done(q):
        for h in range(2):
            for copy in gather_copies(q, h)[0]:
                copy.wait_send()

    def sums(count, fetch, base):
        def step(i, run):
            terms = []
            for u in range(U):
                k = base + (i * U + u) * 8
                tile, keep, lefts, rights = fetch(k)
                terms.append((keep, connection(tile, lefts, rights)))
            for u, (keep, term) in enumerate(terms):
                run = run * keep + term
                S[i * U + u] = run
            return run

        zero = jnp.zeros((C * A, A), F)
        if count == U:
            step(0, zero)
        else:
            lax.fori_loop(0, count // U, step, zero)

    def picked(last, some, i):
        return S[table[last + i]] * table[some + i].astype(F)

    def fetch_f(q):
        def fetch(k):
            tile = G[q][table[k], table[k + 1], table[k + 2]]
            pairs = [table[k + 3 + j] for j in range(3)]
            return tile, table[k + 6].astype(F), [LF[p] for p in pairs], [RF[p] for p in pairs]

        return fetch

    def core_copy(q, t):
        x, z, y = role(q)
        row = up(y, step_of(t))
        return remote(Out.at[q, pl.ds((row * 2 + other) * 8, 8)], RecvC.at[q, row], c_s.at[q, t], c_r.at[q, t], core)

    def core_recv(q, t):
        x, z, y = role(q)
        row = up(y, step_of(t))
        return remote(RecvC.at[q, row], RecvC.at[q, row], c_s.at[q, t], c_r.at[q, t], core)

    def y_copy(q, t):
        x, z, y = role(q)
        row = up(y, step_of(t))
        return remote(
            Out.at[q, pl.ds((row * 2 + c) * 8, 8)], RecvY.at[q, t], y_s.at[q, t], y_r.at[q, t], at_role(q, x, z, row)
        )

    def y_recv(q, t):
        return remote(RecvY.at[q, t], RecvY.at[q, t], y_s.at[q, t], y_r.at[q, t], core)

    def forward_other(q, t):
        x, z, y = role(q)
        row = up(y, step_of(t))
        target = row * 2 + other
        sums(16, fetch_f(q), FWD[q] + target * 128)
        for e in range(8):
            Out[q, target * 8 + e] = picked(LAST_F[q], SOME_F[q], target * 8 + e).astype(BF).reshape(C, A, A)
        core_copy(q, t).start()

    def forward_same(q, t, send):
        x, z, y = role(q)
        row = up(y, step_of(t))
        target = row * 2 + c
        sums(16, fetch_f(q), FWD[q] + target * 128)
        core_recv(q, t).wait_recv()
        for e in range(8):
            total = picked(LAST_F[q], SOME_F[q], target * 8 + e).reshape(C, A, A) + RecvC[q, row, e].astype(F)
            if send:
                Out[q, target * 8 + e] = total.astype(BF)
            else:
                sigma[q, e] = total
        if send:
            y_copy(q, t).start()

    def loop(n, body):
        def run(t, carry):
            body(t)
            return carry

        lax.fori_loop(0, n, run, 0)

    def finish_sigma(q):
        _, _, y = role(q)

        for t in range(3):
            y_recv(q, t).wait_recv()

        def one(e):
            total = sigma[q, e] + RecvY[q, 0, e].astype(F) + RecvY[q, 1, e].astype(F) + RecvY[q, 2, e].astype(F)
            sigma[q, e] = total
            amp = (total / den[e, pl.ds(q * C, C)]).astype(BF)
            Amp[q][y, c, e] = amp
            amps[e, pl.ds(q * C, C)] = amp

        loop(8, one)

    def amp_copies(q):
        _, _, y = role(q)
        to = ys(q)

        def sems(k):
            return ga_s.at[q, k], ga_r.at[q, k]

        def block(d, e):
            return Amp[q].at[up(y, d), c, e]

        first, second = pl.ds(0, 4), pl.ds(4, 4)

        def theirs(d):
            return Amp[q].at[up(y, d), other]

        def mine(d):
            return Amp[q].at[up(y, d), c]

        sends = [
            remote(block(0, first), block(0, first), *sems(0), to[1]),
            remote(block(0, second), block(0, second), *sems(1), to[3]),
            remote(block(0, second), block(0, second), *sems(2), to[1]),
            remote(block(0, first), block(0, first), *sems(3), to[3]),
            remote(block(3, first), block(3, first), *sems(4), to[1]),
            remote(block(1, second), block(1, second), *sems(5), to[3]),
        ] + [remote(mine(d), mine(d), *sems(6 + d), core) for d in range(4)]
        landed = [block(3, first), block(1, second), block(3, second), block(1, first)]
        landed += [block(2, first), block(2, second)] + [theirs(d) for d in range(4)]
        recvs = [remote(b, b, *sems(k), core) for k, b in enumerate(landed)]
        return sends, recvs

    def amp_step(q, step):
        sends, recvs = amp_copies(q)
        if step == 0:
            for k in (0, 1, 2, 3, 6):
                sends[k].start()
        if step == 1:
            recvs[0].wait_recv()
            sends[4].start()
            recvs[1].wait_recv()
            sends[5].start()
        if step == 2:
            recvs[2].wait_recv()
            sends[9].start()
            recvs[3].wait_recv()
            sends[7].start()
            recvs[4].wait_recv()
            recvs[5].wait_recv()
            sends[8].start()
        if step == 3:
            for k in range(6, 10):
                recvs[k].wait_recv()

    def amp_done(q):
        for copy in amp_copies(q)[0]:
            copy.wait_send()

    def fetch_b(q):
        def fetch(k):
            tile = Amp[q][table[k], table[k + 1], table[k + 2]]
            pairs = [table[k + 3 + j] for j in range(3)]
            return tile, table[k + 6].astype(F), [LB[p] for p in pairs], [RB[p] for p in pairs]

        return fetch

    def z_copy(q, a, b):
        x, z, y = role(q)
        iz, ix = up(z, step_of(a)), up(x, step_of(b))
        return remote(
            Out.at[q, pl.ds((ix * 4 + iz) * 4, 2)], RecvZ.at[q, a, ix], z_s.at[q, a], z_r.at[q, a],
            at_role(q, x, iz, y),
        )

    def x_copy(q, a, b):
        x, z, y = role(q)
        iz, ix = up(z, step_of(a)), up(x, step_of(b))
        return remote(
            Out.at[q, pl.ds((ix * 4 + iz) * 4 + 2, 2)], RecvX.at[q, b, iz], x_s.at[q, b], x_r.at[q, b],
            at_role(q, ix, z, y),
        )

    def backward(q, t, held=False):
        a, b = lax.div(t, 4), lax.rem(t, 4)
        x, z, _ = role(q)
        target = up(x, step_of(b)) * 4 + up(z, step_of(a))
        sums(8, fetch_b(q), BWD[q] + target * 64)
        for v in range(4):
            Out[q, target * 4 + v] = picked(LAST_B[q], SOME_B[q], target * 4 + v).astype(BF).reshape(C, A, A)

        @pl.when(a < 3)
        def _():
            z_copy(q, a, b).start()

        if not held:

            @pl.when(b < 3)
            def _():
                x_copy(q, a, b).start()

    def release(q):
        def one(t):
            a, b = lax.div(t, 3), lax.rem(t, 3)
            x_copy(q, a, b).start()

        loop(9, one)

    def z2_copy(q, i):
        x, z, y = role(q)
        ix = up(x, step_of(i))
        return remote(
            Out.at[q, pl.ds((ix * 4 + z) * 4, 2)], RecvZ2.at[q, i], z2_s.at[q, i], z2_r.at[q, i],
            at_role(q, ix, z, y),
        )

    def x2_copy(q, i):
        x, z, y = role(q)
        iz = up(z, step_of(i))
        return remote(
            Out.at[q, pl.ds((x * 4 + iz) * 4 + 2, 2)], RecvX2.at[q, i], x2_s.at[q, i], x2_r.at[q, i],
            at_role(q, x, iz, y),
        )

    def whole(buffer, send, recv):
        return remote(buffer, buffer, send, recv, core)

    def second_stage(q):
        x, z, _ = role(q)
        for a in range(3):
            whole(RecvZ.at[q, a], z_s.at[q, a], z_r.at[q, a]).wait_recv()
            whole(RecvX.at[q, a], x_s.at[q, a], x_r.at[q, a]).wait_recv()

        def total(at, recv, i, v):
            return Out[q, at + v].astype(F) + recv[q, 0, i, v].astype(F) + recv[q, 1, i, v].astype(F) + recv[q, 2, i, v].astype(F)

        def one(i):
            ix, iz = up(x, step_of(i)), up(z, step_of(i))
            at_z, at_x = (ix * 4 + z) * 4, (x * 4 + iz) * 4 + 2
            for v in range(2):
                Out[q, at_z + v] = total(at_z, RecvZ, ix, v).astype(BF)
            z2_copy(q, i).start()
            for v in range(2):
                Out[q, at_x + v] = total(at_x, RecvX, iz, v).astype(BF)
            x2_copy(q, i).start()

        loop(3, one)
        at = (x * 4 + z) * 4
        for v in range(2):
            dress[v, pl.ds(q * C, C)] = total(at, RecvZ, x, v)
            dress[2 + v, pl.ds(q * C, C)] = total(at + 2, RecvX, z, v)

    def last_stage(q):
        for i in range(3):
            whole(RecvZ2.at[q, i], z2_s.at[q, i], z2_r.at[q, i]).wait_recv()
            whole(RecvX2.at[q, i], x2_s.at[q, i], x2_r.at[q, i]).wait_recv()
        for v in range(2):
            for at, recv in ((v, RecvZ2), (2 + v, RecvX2)):
                dress[at, pl.ds(q * C, C)] = dress[at, pl.ds(q * C, C)] + (
                    recv[q, 0, v].astype(F) + recv[q, 1, v].astype(F) + recv[q, 2, v].astype(F)
                )

    def local_gram():
        def one(e, total):
            sig = [sigma[s // C, e, s % C] for s in range(4)]
            amp = [amps[e, s].astype(F) for s in range(4)]
            return tuple(
                total[s * 4 + t] + (sig[s] * amp[t]).reshape(16, 8, A).sum(axis=0)
                for s in range(4)
                for t in range(4)
            )

        sums_ = lax.fori_loop(0, 8, one, tuple(jnp.zeros((8, A), F) for _ in range(16)))
        row = lax.broadcasted_iota(jnp.int32, (8, A), 0)
        col = lax.broadcasted_iota(jnp.int32, (8, A), 1)
        out = jnp.zeros((8, A), F)
        for s in range(4):
            for t in range(4):
                value = jnp.sum(sums_[s * 4 + t]) / (1024.0 * A * A)
                out = out + jnp.where((row == s) & (col == t), value, 0.0)
        own_gram[0] = out

    gram_axes = ((0, 3, xs(0)), (3, 3, zs(0)), (6, 3, ys(0)), (9, 1, [None, core]))

    def gram_send(k):
        first, n, devs = gram_axes[k]
        for i in range(n):
            remote(own_gram.at[k], peer_gram.at[first + i], gr_s.at[first + i], gr_r.at[first + i], devs[1 + i]).start()

    def gram_take(k):
        first, n, _ = gram_axes[k]
        out = own_gram[k]
        for i in range(n):
            whole(peer_gram.at[first + i], gr_s.at[first + i], gr_r.at[first + i]).wait_recv()
            out = out + peer_gram[first + i]
        own_gram[k + 1] = out

    def forward(q, n, first):
        def both(t):
            forward_other(q, t)
            forward_same(q, t, True)

        loop(n, lambda t: both(t + first))

    def forward_last(q):
        forward_other(q, 3)
        forward_same(q, 3, False)

    gather_step(0, 0)
    gather_step(1, 0)
    gather_step(0, 1)
    gather_step(1, 1)
    own_tiles(0).wait()
    own_tiles(1).wait()
    gather_step(0, 2)
    gather_step(1, 2, (1,))
    for load in loads:
        load.wait()
    turn(LB, LF)
    gather_step(0, 3)
    gather_step(1, 3, (1,))
    turn(RF, RB)
    gather_step(0, 4)
    gather_step(1, 2, (0,))
    forward(0, 2, 0)
    gather_step(1, 3, (0,))
    forward(0, 1, 2)
    forward_last(0)
    gather_step(1, 4)
    forward(1, 2, 0)
    finish_sigma(0)
    amp_step(0, 0)
    forward(1, 1, 2)
    amp_step(0, 1)
    forward_last(1)
    for t in range(4):
        core_copy(0, t).wait_send()
    for t in range(3):
        y_copy(0, t).wait_send()
    amp_step(0, 2)
    amp_step(0, 3)
    loop(2, lambda t: backward(0, t, True))
    finish_sigma(1)
    amp_step(1, 0)
    local_gram()
    gram_send(0)
    loop(5, lambda t: backward(0, t + 2, True))
    amp_step(1, 1)
    gram_take(0)
    gram_send(1)
    loop(5, lambda t: backward(0, t + 7, True))
    amp_step(1, 2)
    release(0)
    gram_take(1)
    gram_send(2)
    loop(4, lambda t: backward(0, t + 12))
    gram_take(2)
    gram_send(3)
    for t in range(4):
        core_copy(1, t).wait_send()
    for t in range(3):
        y_copy(1, t).wait_send()
    amp_step(1, 3)
    loop(13, lambda t: backward(1, t))
    for a in range(3):
        whole(RecvZ.at[0, a], z_s.at[0, a], z_r.at[0, a]).wait_send()
        whole(RecvX.at[0, a], x_s.at[0, a], x_r.at[0, a]).wait_send()
    second_stage(0)
    loop(3, lambda t: backward(1, t + 13))
    last_stage(0)
    gram_take(3)
    gram[...] = own_gram[4]
    for a in range(3):
        whole(RecvZ.at[1, a], z_s.at[1, a], z_r.at[1, a]).wait_send()
        whole(RecvX.at[1, a], x_s.at[1, a], x_r.at[1, a]).wait_send()
    second_stage(1)
    last_stage(1)
    for q in range(Q):
        gather_done(q)
        amp_done(q)
        for i in range(3):
            z2_copy(q, i).wait_send()
            x2_copy(q, i).wait_send()
    for k in range(10):
        whole(peer_gram.at[k], gr_s.at[k], gr_r.at[k]).wait_send()


def run_main(table, coefficients, alpha, beta, denominators):
    dma = pltpu.SemaphoreType.DMA
    tiles = lambda *n: pltpu.VMEM((*n, C, A, A), BF)
    factor = pltpu.VMEM((64, A, A), BF)
    return pl.pallas_call(
        main_kernel,
        out_shape=(
            jax.ShapeDtypeStruct((8, 4, A, A), BF),
            jax.ShapeDtypeStruct((4, 4, A, A), F),
            jax.ShapeDtypeStruct((8, A), F),
        ),
        in_specs=[pl.BlockSpec(memory_space=pltpu.SMEM)] + [pl.BlockSpec(memory_space=pl.ANY)] * 4,
        out_specs=[pl.BlockSpec(memory_space=pltpu.VMEM)] * 3,
        scratch_shapes=[
            tiles(4, 4, 4), tiles(4, 4, 4),
            factor, factor, factor, factor,
            pltpu.VMEM((8, 4, A, A), F),
            pltpu.VMEM((16, C * A, A), F),
            tiles(Q, 64),
            tiles(Q, 4, 8),
            tiles(Q, 3, 8),
            pltpu.VMEM((Q, 8, C, A, A), F),
            tiles(4, 2, 8), tiles(4, 2, 8),
            tiles(Q, 3, 4, 2),
            tiles(Q, 3, 4, 2),
            tiles(Q, 3, 2),
            tiles(Q, 3, 2),
            pltpu.VMEM((5, 8, A), F),
            pltpu.VMEM((10, 8, A), F),
            dma((5,)),
            dma((Q, 2, 12)), dma((Q, 2, 12)),
            dma((Q, 4)), dma((Q, 4)),
            dma((Q, 3)), dma((Q, 3)),
            dma((Q, 10)), dma((Q, 10)),
            dma((Q, 3)), dma((Q, 3)), dma((Q, 3)), dma((Q, 3)),
            dma((Q, 3)), dma((Q, 3)), dma((Q, 3)), dma((Q, 3)),
            dma((10,)), dma((10,)),
        ],
        compiler_params=pltpu.CompilerParams(
            collective_id=1, has_side_effects=True, vmem_limit_bytes=60 * 2**20
        ),
    )(table, coefficients, alpha, beta, denominators)


def in_order(key, fields, targets):
    k = key.shape[1]
    at = jnp.arange(k, dtype=jnp.int32)
    before = (key[:, :, None] > key[:, None, :]) | (
        (key[:, :, None] == key[:, None, :]) & (at[:, None] > at[None, :])
    )
    rank = jnp.sum(before.astype(jnp.int32), axis=2)
    onehot = (rank[:, None, :] == at[None, :, None]).astype(jnp.int32)
    full = jnp.concatenate([fields, key[:, :, None]], axis=2)
    ordered = jnp.sum(onehot[:, :, :, None] * full[:, None, :, :], axis=2)
    key = ordered[:, :, 6]
    keep = (key == jnp.concatenate([jnp.full_like(key[:, :1], -1), key[:, :-1]], axis=1)).astype(jnp.int32)
    ordered = jnp.concatenate([ordered[:, :, :6], keep[:, :, None], keep[:, :, None]], axis=2)
    values = jnp.arange(targets, dtype=jnp.int32)
    last = jnp.sum((key[:, :, None] <= values).astype(jnp.int32), axis=1) - 1
    some = jnp.sum((key[:, :, None] == values).astype(jnp.int32), axis=1) > 0
    return ordered, jnp.maximum(last, 0), some.astype(jnp.int32)


def per_device(coefficients, send_tile, slot_external, slot_pairs, factor_alpha, factor_beta, denominators):
    own = jnp.concatenate(
        [send_tile, slot_external, slot_pairs[0].T, jnp.zeros((3, 128), jnp.int32)], axis=0
    )
    planes, rings = exchange_tables(own)
    x, z, y, c = place()
    pick = lax.dynamic_index_in_dim

    tile_0 = pick(planes[0, :, 0].reshape(16, 16, 8), x * 4 + z, 1, False).T
    tile_1 = pick(planes[1, :, 0].reshape(16, 4, 16, 2), z * 4 + y, 2, False).reshape(16, 8).T
    mine_0 = pick(rings[0].reshape(8, 8, 16, 8), y * 2 + c, 3, False)
    mine_1 = pick(pick(rings[1].reshape(8, 8, 4, 4, 4, 2), x, 2, False), c, 4, False)
    mine_1 = mine_1.swapaxes(2, 3).reshape(8, 8, 16)
    tile = jnp.stack([tile_0, tile_1])
    mine = jnp.stack([mine_0, mine_1])
    external = mine[:, :, 1]
    pairs = mine[:, :, 2:5].transpose(0, 1, 3, 2)
    owner = jnp.arange(16, dtype=jnp.int32)
    receiver = jnp.arange(8, dtype=jnp.int32)

    def fields(index, width, count, value, pairs):
        spread = lambda a: jnp.broadcast_to(a, (2 * count, len(index)))[:, :, None]
        value = value.reshape(2 * count, len(index), 1)
        return jnp.concatenate(
            [spread(index // width), spread(index % width), value, pairs.reshape(2 * count, len(index), 3)],
            axis=2,
        )

    fields_f = fields(owner, 4, 8, tile, pairs)
    fields_b = fields(receiver, 2, 16, external.swapaxes(1, 2), pairs.swapaxes(1, 2))
    parts = [
        *in_order(external.reshape(16, 16), fields_f, 8),
        *in_order(tile.swapaxes(1, 2).reshape(32, 8), fields_b, 4),
    ]
    table = jnp.concatenate([parts[i].reshape(-1) for i in (0, 3, 1, 2, 4, 5)])
    amplitudes, dressing, gram = run_main(table, coefficients, factor_alpha, factor_beta, denominators)
    return amplitudes, dressing, gram[:4, :4]


def solution(mesh):
    return jax.shard_map(
        per_device,
        mesh=mesh,
        in_specs=(
            P("dev", None, None, None),
            P("dev", None),
            P("dev", None),
            P("dev", None, None),
            P(),
            P(),
            P("dev", None, None, None),
        ),
        out_specs=(P("dev", None, None, None), P("dev", None, None, None), P()),
        check_vma=False,
    )
```

```python
import functools

import jax
import jax.numpy as jnp
from jax import lax
from jax.experimental import pallas as pl
from jax.experimental.pallas import tpu as pltpu
from jax.sharding import PartitionSpec as P

BF = jnp.bfloat16
F = jnp.float32
MESH = pl.DeviceIdType.MESH
A = 128
C = 2
Q = 2
U = 8
FWD, BWD = (0, 1024), (2048, 3072)
LAST_F, SOME_F = (4096, 4160), (4224, 4288)
LAST_B, SOME_B = (4352, 4416), (4480, 4544)


def place():
    me = lax.axis_index("dev")
    return lax.div(me, 32), lax.rem(lax.div(me, 8), 4), lax.rem(lax.div(me, 2), 4), lax.rem(me, 2)


def device(x, z, y, c):
    return ((x * 4 + z) * 4 + y) * 2 + c


def up(i, d):
    return lax.rem(i + d, 4)


def step_of(t):
    if isinstance(t, int):
        return (2, 1, 3, 0)[t]
    return jnp.where(t == 0, 2, jnp.where(t == 3, 0, 2 * t - 1))


class remote:
    def __init__(self, src, dst, send, recv, to):
        self.what = (src, dst, send, recv, to)

    def copy(self):
        src, dst, send, recv, to = self.what
        return pltpu.make_async_remote_copy(
            src_ref=src, dst_ref=dst, send_sem=send, recv_sem=recv, device_id=(to,), device_id_type=MESH
        )

    def start(self):
        self.copy().start()

    def wait_send(self):
        self.copy().wait_send()

    def wait_recv(self):
        self.copy().wait_recv()


def greet(peers):
    barrier = pltpu.get_barrier_semaphore()
    for p in peers:
        pl.semaphore_signal(barrier, inc=1, device_id=(p,), device_id_type=MESH)
    pl.semaphore_wait(barrier, len(peers))


STEPS = [
    (dx, dz, dy, dc)
    for dx in range(4)
    for dz in range(4)
    for dy in range(4)
    for dc in range(2)
    if (dy, dc) == (0, 0) or (dx, dz) == (0, 0) or (dx, dc) == (0, 0) or (dz, dy) == (0, 0)
]


def table_kernel(own, planes, rings, rows, send, recv):
    x, z, y, c = place()

    def to(d):
        return up(x, d[0]), up(z, d[1]), up(y, d[2]), lax.rem(c + d[3], 2)

    others = STEPS[1:]
    greet([device(*to(d)) for d in others])
    copies = [
        remote(own, rows.at[i], send.at[i], recv.at[i], device(*to(d))) for i, d in enumerate(others)
    ]
    for copy in copies:
        copy.start()
    for i, d in enumerate(STEPS):
        if i:
            copies[i - 1].wait_recv()
        row = own[...] if i == 0 else rows[i - 1]
        fx, fz, fy, fc = to([4 - v for v in d])
        if d[2] == 0 and d[3] == 0:
            planes[0, fx * 4 + fz] = row
        if d[0] == 0 and d[1] == 0:
            rings[0, fy * 2 + fc] = row
        if d[0] == 0 and d[3] == 0:
            planes[1, fy * 4 + fz] = row
        if d[1] == 0 and d[2] == 0:
            rings[1, fx * 2 + fc] = row
    for copy in copies:
        copy.wait_send()


def exchange_tables(own):
    n = len(STEPS) - 1
    return pl.pallas_call(
        table_kernel,
        out_shape=(
            jax.ShapeDtypeStruct((2, 16, 8, 128), jnp.int32),
            jax.ShapeDtypeStruct((2, 8, 8, 128), jnp.int32),
        ),
        in_specs=[pl.BlockSpec(memory_space=pltpu.VMEM)],
        out_specs=[pl.BlockSpec(memory_space=pltpu.VMEM)] * 2,
        scratch_shapes=[
            pltpu.VMEM((n, 8, 128), jnp.int32),
            pltpu.SemaphoreType.DMA((n,)),
            pltpu.SemaphoreType.DMA((n,)),
        ],
        compiler_params=pltpu.CompilerParams(collective_id=0, has_side_effects=True),
    )(own)


def dot(a, b):
    return jnp.dot(a, b, preferred_element_type=F)


def connection(tile, left, right):
    wide = jnp.concatenate([tile[s] for s in range(C)], axis=1)
    half = dot(jnp.concatenate(left, axis=0), wide).astype(BF)
    rows = [
        jnp.concatenate(
            [half[j * A : (j + 1) * A, s * A : (s + 1) * A] for j in range(len(left))], axis=1
        )
        for s in range(C)
    ]
    return dot(jnp.concatenate(rows, axis=0), jnp.concatenate(right, axis=0))


def main_kernel(
    table, coef, alpha, beta, den_hbm,
    amps, dress, gram,
    G0, G1, LF, RF, LB, RB, den, S, Out, RecvC, RecvY, sigma, Amp0, Amp1, RecvZ, RecvX, RecvZ2, RecvX2,
    own_gram, peer_gram, loc, ag_s, ag_r, c_s, c_r, y_s, y_r, ga_s, ga_r, z_s, z_r, x_s, x_r,
    z2_s, z2_r, x2_s, x2_r, gr_s, gr_r,
):
    px, pz, py, c = place()
    G, Amp = (G0, G1), (Amp0, Amp1)
    other = 1 - c
    core = device(px, pz, py, other)

    def role(q):
        return (px, pz, py) if q == 0 else (py, pz, px)

    def at_role(q, x, z, y):
        return device(x, z, y, c) if q == 0 else device(y, z, x, c)

    def xs(q):
        x, z, y = role(q)
        return [at_role(q, up(x, d), z, y) for d in range(4)]

    def zs(q):
        x, z, y = role(q)
        return [at_role(q, x, up(z, d), y) for d in range(4)]

    def ys(q):
        x, z, y = role(q)
        return [at_role(q, x, z, up(y, d)) for d in range(4)]

    def own_tiles(q):
        x, z, _ = role(q)
        return pltpu.make_async_copy(coef.at[:, pl.ds(q * C, C)], G[q].at[x, z], loc.at[q])

    loads = [
        pltpu.make_async_copy(src, dst, loc.at[2 + i])
        for i, (src, dst) in enumerate([(alpha, LB), (beta, RF), (den_hbm, den)])
    ]
    for q in range(Q):
        own_tiles(q).start()
    for load in loads:
        load.start()
    greet(xs(0)[1:] + zs(0)[1:] + ys(0)[1:] + [core])

    def turn(src, dst):
        def step(i, carry):
            for u in range(4):
                dst[i * 4 + u] = src[i * 4 + u].T
            return carry

        lax.fori_loop(0, 16, step, 0)

    def gather_copies(q, h):
        x, z, _ = role(q)
        lo = 2 * h
        near, far = (xs(q), zs(q)) if h == 0 else (zs(q), xs(q))
        first, second, both = pl.ds(lo, 1), pl.ds(lo + 1, 1), pl.ds(lo, 2)

        def block(d, e, tiles):
            dx, dz = (d, e) if h == 0 else (e, d)
            ix = pl.ds(0, 4) if dx is None else up(x, dx)
            iz = pl.ds(0, 4) if dz is None else up(z, dz)
            return G[q].at[ix, iz, tiles]

        def sems(k):
            return ag_s.at[q, h, k], ag_r.at[q, h, k]

        sends, landed = [], []
        for stage in range(2):
            to = (near, far)[stage]

            def at(d, tiles):
                return block(d, 0, tiles) if stage == 0 else block(None, d, tiles)

            def source(tiles):
                return coef.at[tiles, pl.ds(q * C, C)] if stage == 0 else at(0, tiles)

            k = 6 * stage
            sends += [
                remote(source(first), at(0, first), *sems(k), to[1]),
                remote(source(second), at(0, second), *sems(k + 1), to[3]),
                remote(source(second), at(0, second), *sems(k + 2), to[1]),
                remote(source(first), at(0, first), *sems(k + 3), to[3]),
                remote(at(3, first), at(3, first), *sems(k + 4), to[1]),
                remote(at(1, second), at(1, second), *sems(k + 5), to[3]),
            ]
            landed += [at(3, first), at(1, second), at(3, second), at(1, first), at(2, first), at(2, second)]
        recvs = [remote(b, b, *sems(k), near[1]) for k, b in enumerate(landed)]
        return sends, recvs

    def gather_step(q, step, halves=(0, 1)):
        for h in halves:
            sends, recvs = gather_copies(q, h)
            if step in (1, 3):
                k = 6 * (step // 2)
                for i in range(2):
                    recvs[k + i].wait_recv()
                    sends[k + 4 + i].start()
            else:
                if step:
                    for k in range(2, 6):
                        recvs[3 * step - 6 + k].wait_recv()
                if step < 4:
                    for k in range(4):
                        sends[3 * step + k].start()

    def gather_done(q):
        for h in range(2):
            for copy in gather_copies(q, h)[0]:
                copy.wait_send()

    def sums(count, fetch, base):
        def step(i, run):
            terms = []
            for u in range(U):
                k = base + (i * U + u) * 8
                tile, keep, lefts, rights = fetch(k)
                terms.append((keep, connection(tile, lefts, rights)))
            for u, (keep, term) in enumerate(terms):
                run = run * keep + term
                S[i * U + u] = run
            return run

        zero = jnp.zeros((C * A, A), F)
        if count == U:
            step(0, zero)
        else:
            lax.fori_loop(0, count // U, step, zero)

    def picked(last, some, i):
        return S[table[last + i]] * table[some + i].astype(F)

    def fetch_f(q):
        def fetch(k):
            tile = G[q][table[k], table[k + 1], table[k + 2]]
            pairs = [table[k + 3 + j] for j in range(3)]
            return tile, table[k + 6].astype(F), [LF[p] for p in pairs], [RF[p] for p in pairs]

        return fetch

    def core_copy(q, t):
        x, z, y = role(q)
        row = up(y, step_of(t))
        return remote(Out.at[q, pl.ds((row * 2 + other) * 8, 8)], RecvC.at[q, row], c_s.at[q, t], c_r.at[q, t], core)

    def core_recv(q, t):
        x, z, y = role(q)
        row = up(y, step_of(t))
        return remote(RecvC.at[q, row], RecvC.at[q, row], c_s.at[q, t], c_r.at[q, t], core)

    def y_copy(q, t):
        x, z, y = role(q)
        row = up(y, step_of(t))
        return remote(
            Out.at[q, pl.ds((row * 2 + c) * 8, 8)], RecvY.at[q, t], y_s.at[q, t], y_r.at[q, t], at_role(q, x, z, row)
        )

    def y_recv(q, t):
        return remote(RecvY.at[q, t], RecvY.at[q, t], y_s.at[q, t], y_r.at[q, t], core)

    def forward_other(q, t):
        x, z, y = role(q)
        row = up(y, step_of(t))
        target = row * 2 + other
        sums(16, fetch_f(q), FWD[q] + target * 128)
        for e in range(8):
            Out[q, target * 8 + e] = picked(LAST_F[q], SOME_F[q], target * 8 + e).astype(BF).reshape(C, A, A)
        core_copy(q, t).start()

    def forward_same(q, t, send):
        x, z, y = role(q)
        row = up(y, step_of(t))
        target = row * 2 + c
        sums(16, fetch_f(q), FWD[q] + target * 128)
        core_recv(q, t).wait_recv()
        for e in range(8):
            total = picked(LAST_F[q], SOME_F[q], target * 8 + e).reshape(C, A, A) + RecvC[q, row, e].astype(F)
            if send:
                Out[q, target * 8 + e] = total.astype(BF)
            else:
                sigma[q, e] = total
        if send:
            y_copy(q, t).start()

    def loop(n, body):
        def run(t, carry):
            body(t)
            return carry

        lax.fori_loop(0, n, run, 0)

    def finish_sigma(q):
        _, _, y = role(q)

        for t in range(3):
            y_recv(q, t).wait_recv()

        def one(e):
            total = sigma[q, e] + RecvY[q, 0, e].astype(F) + RecvY[q, 1, e].astype(F) + RecvY[q, 2, e].astype(F)
            sigma[q, e] = total
            amp = (total / den[e, pl.ds(q * C, C)]).astype(BF)
            Amp[q][y, c, e] = amp
            amps[e, pl.ds(q * C, C)] = amp

        loop(8, one)

    def amp_copies(q):
        _, _, y = role(q)
        to = ys(q)

        def sems(k):
            return ga_s.at[q, k], ga_r.at[q, k]

        def block(d, e):
            return Amp[q].at[up(y, d), c, e]

        first, second = pl.ds(0, 4), pl.ds(4, 4)

        def theirs(d):
            return Amp[q].at[up(y, d), other]

        def mine(d):
            return Amp[q].at[up(y, d), c]

        sends = [
            remote(block(0, first), block(0, first), *sems(0), to[1]),
            remote(block(0, second), block(0, second), *sems(1), to[3]),
            remote(block(0, second), block(0, second), *sems(2), to[1]),
            remote(block(0, first), block(0, first), *sems(3), to[3]),
            remote(block(3, first), block(3, first), *sems(4), to[1]),
            remote(block(1, second), block(1, second), *sems(5), to[3]),
        ] + [remote(mine(d), mine(d), *sems(6 + d), core) for d in range(4)]
        landed = [block(3, first), block(1, second), block(3, second), block(1, first)]
        landed += [block(2, first), block(2, second)] + [theirs(d) for d in range(4)]
        recvs = [remote(b, b, *sems(k), core) for k, b in enumerate(landed)]
        return sends, recvs

    def amp_step(q, step):
        sends, recvs = amp_copies(q)
        if step == 0:
            for k in (0, 1, 2, 3, 6):
                sends[k].start()
        if step == 1:
            recvs[0].wait_recv()
            sends[4].start()
            recvs[1].wait_recv()
            sends[5].start()
        if step == 2:
            recvs[2].wait_recv()
            sends[9].start()
            recvs[3].wait_recv()
            sends[7].start()
            recvs[4].wait_recv()
            recvs[5].wait_recv()
            sends[8].start()
        if step == 3:
            for k in range(6, 10):
                recvs[k].wait_recv()

    def amp_done(q):
        for copy in amp_copies(q)[0]:
            copy.wait_send()

    def fetch_b(q):
        def fetch(k):
            tile = Amp[q][table[k], table[k + 1], table[k + 2]]
            pairs = [table[k + 3 + j] for j in range(3)]
            return tile, table[k + 6].astype(F), [LB[p] for p in pairs], [RB[p] for p in pairs]

        return fetch

    def z_copy(q, a, b):
        x, z, y = role(q)
        iz, ix = up(z, step_of(a)), up(x, step_of(b))
        return remote(
            Out.at[q, pl.ds((ix * 4 + iz) * 4, 2)], RecvZ.at[q, a, ix], z_s.at[q, a], z_r.at[q, a],
            at_role(q, x, iz, y),
        )

    def x_copy(q, a, b):
        x, z, y = role(q)
        iz, ix = up(z, step_of(a)), up(x, step_of(b))
        return remote(
            Out.at[q, pl.ds((ix * 4 + iz) * 4 + 2, 2)], RecvX.at[q, b, iz], x_s.at[q, b], x_r.at[q, b],
            at_role(q, ix, z, y),
        )

    def backward(q, t, held=False):
        a, b = lax.div(t, 4), lax.rem(t, 4)
        x, z, _ = role(q)
        target = up(x, step_of(b)) * 4 + up(z, step_of(a))
        sums(8, fetch_b(q), BWD[q] + target * 64)
        for v in range(4):
            Out[q, target * 4 + v] = picked(LAST_B[q], SOME_B[q], target * 4 + v).astype(BF).reshape(C, A, A)

        @pl.when(a < 3)
        def _():
            z_copy(q, a, b).start()

        if not held:

            @pl.when(b < 3)
            def _():
                x_copy(q, a, b).start()

    def release(q):
        def one(t):
            a, b = lax.div(t, 3), lax.rem(t, 3)
            x_copy(q, a, b).start()

        loop(9, one)

    def z2_copy(q, i):
        x, z, y = role(q)
        ix = up(x, step_of(i))
        return remote(
            Out.at[q, pl.ds((ix * 4 + z) * 4, 2)], RecvZ2.at[q, i], z2_s.at[q, i], z2_r.at[q, i],
            at_role(q, ix, z, y),
        )

    def x2_copy(q, i):
        x, z, y = role(q)
        iz = up(z, step_of(i))
        return remote(
            Out.at[q, pl.ds((x * 4 + iz) * 4 + 2, 2)], RecvX2.at[q, i], x2_s.at[q, i], x2_r.at[q, i],
            at_role(q, x, iz, y),
        )

    def whole(buffer, send, recv):
        return remote(buffer, buffer, send, recv, core)

    def second_stage(q):
        x, z, _ = role(q)
        def total(at, recv, i, v):
            return Out[q, at + v].astype(F) + recv[q, 0, i, v].astype(F) + recv[q, 1, i, v].astype(F) + recv[q, 2, i, v].astype(F)

        def one_z(i):
            ix = up(x, step_of(i))
            at = (ix * 4 + z) * 4
            for v in range(2):
                Out[q, at + v] = total(at, RecvZ, ix, v).astype(BF)
            z2_copy(q, i).start()

        def one_x(i):
            iz = up(z, step_of(i))
            at = (x * 4 + iz) * 4 + 2
            for v in range(2):
                Out[q, at + v] = total(at, RecvX, iz, v).astype(BF)
            x2_copy(q, i).start()

        for a in range(3):
            whole(RecvZ.at[q, a], z_s.at[q, a], z_r.at[q, a]).wait_recv()
        loop(3, one_z)
        for a in range(3):
            whole(RecvX.at[q, a], x_s.at[q, a], x_r.at[q, a]).wait_recv()
        loop(3, one_x)
        at = (x * 4 + z) * 4
        for v in range(2):
            dress[v, pl.ds(q * C, C)] = total(at, RecvZ, x, v)
            dress[2 + v, pl.ds(q * C, C)] = total(at + 2, RecvX, z, v)

    def last_stage(q):
        for i in range(3):
            whole(RecvZ2.at[q, i], z2_s.at[q, i], z2_r.at[q, i]).wait_recv()
            whole(RecvX2.at[q, i], x2_s.at[q, i], x2_r.at[q, i]).wait_recv()
        for v in range(2):
            for at, recv in ((v, RecvZ2), (2 + v, RecvX2)):
                dress[at, pl.ds(q * C, C)] = dress[at, pl.ds(q * C, C)] + (
                    recv[q, 0, v].astype(F) + recv[q, 1, v].astype(F) + recv[q, 2, v].astype(F)
                )

    def local_gram():
        def one(e, total):
            sig = [sigma[s // C, e, s % C] for s in range(4)]
            amp = [amps[e, s].astype(F) for s in range(4)]
            return tuple(
                total[s * 4 + t] + (sig[s] * amp[t]).reshape(16, 8, A).sum(axis=0)
                for s in range(4)
                for t in range(4)
            )

        sums_ = lax.fori_loop(0, 8, one, tuple(jnp.zeros((8, A), F) for _ in range(16)))
        row = lax.broadcasted_iota(jnp.int32, (8, A), 0)
        col = lax.broadcasted_iota(jnp.int32, (8, A), 1)
        out = jnp.zeros((8, A), F)
        for s in range(4):
            for t in range(4):
                value = jnp.sum(sums_[s * 4 + t]) / (1024.0 * A * A)
                out = out + jnp.where((row == s) & (col == t), value, 0.0)
        own_gram[0] = out

    gram_axes = ((0, 3, xs(0)), (3, 3, zs(0)), (6, 3, ys(0)), (9, 1, [None, core]))

    def gram_send(k):
        first, n, devs = gram_axes[k]
        for i in range(n):
            remote(own_gram.at[k], peer_gram.at[first + i], gr_s.at[first + i], gr_r.at[first + i], devs[1 + i]).start()

    def gram_take(k):
        first, n, _ = gram_axes[k]
        out = own_gram[k]
        for i in range(n):
            whole(peer_gram.at[first + i], gr_s.at[first + i], gr_r.at[first + i]).wait_recv()
            out = out + peer_gram[first + i]
        own_gram[k + 1] = out

    def forward(q, n, first):
        def both(t):
            forward_other(q, t)
            forward_same(q, t, True)

        loop(n, lambda t: both(t + first))

    def forward_last(q):
        forward_other(q, 3)
        forward_same(q, 3, False)

    gather_step(0, 0)
    gather_step(1, 0)
    gather_step(0, 1)
    gather_step(1, 1)
    own_tiles(0).wait()
    own_tiles(1).wait()
    gather_step(0, 2)
    gather_step(1, 2, (1,))
    for load in loads:
        load.wait()
    turn(LB, LF)
    gather_step(0, 3)
    gather_step(1, 3, (1,))
    turn(RF, RB)
    gather_step(0, 4)
    gather_step(1, 2, (0,))
    forward(0, 2, 0)
    gather_step(1, 3, (0,))
    forward(0, 1, 2)
    forward_last(0)
    gather_step(1, 4)
    forward(1, 1, 0)
    finish_sigma(0)
    amp_step(0, 0)
    forward(1, 1, 1)
    amp_step(0, 1)
    forward(1, 1, 2)
    forward_last(1)
    for t in range(4):
        core_copy(0, t).wait_send()
    for t in range(3):
        y_copy(0, t).wait_send()
    amp_step(0, 2)
    amp_step(0, 3)
    loop(2, lambda t: backward(0, t, True))
    finish_sigma(1)
    amp_step(1, 0)
    local_gram()
    gram_send(0)
    loop(5, lambda t: backward(0, t + 2, True))
    amp_step(1, 1)
    gram_take(0)
    gram_send(1)
    loop(5, lambda t: backward(0, t + 7, True))
    amp_step(1, 2)
    release(0)
    gram_take(1)
    gram_send(2)
    loop(4, lambda t: backward(0, t + 12))
    gram_take(2)
    gram_send(3)
    for t in range(4):
        core_copy(1, t).wait_send()
    for t in range(3):
        y_copy(1, t).wait_send()
    amp_step(1, 3)
    loop(13, lambda t: backward(1, t))
    for a in range(3):
        whole(RecvZ.at[0, a], z_s.at[0, a], z_r.at[0, a]).wait_send()
        whole(RecvX.at[0, a], x_s.at[0, a], x_r.at[0, a]).wait_send()
    second_stage(0)
    loop(3, lambda t: backward(1, t + 13))
    last_stage(0)
    gram_take(3)
    gram[...] = own_gram[4][:4, :4]
    for a in range(3):
        whole(RecvZ.at[1, a], z_s.at[1, a], z_r.at[1, a]).wait_send()
        whole(RecvX.at[1, a], x_s.at[1, a], x_r.at[1, a]).wait_send()
    second_stage(1)
    last_stage(1)
    for q in range(Q):
        gather_done(q)
        amp_done(q)
        for i in range(3):
            z2_copy(q, i).wait_send()
            x2_copy(q, i).wait_send()
    for k in range(10):
        whole(peer_gram.at[k], gr_s.at[k], gr_r.at[k]).wait_send()


def run_main(table, coefficients, alpha, beta, denominators):
    dma = pltpu.SemaphoreType.DMA
    tiles = lambda *n: pltpu.VMEM((*n, C, A, A), BF)
    factor = pltpu.VMEM((64, A, A), BF)
    return pl.pallas_call(
        main_kernel,
        out_shape=(
            jax.ShapeDtypeStruct((8, 4, A, A), BF),
            jax.ShapeDtypeStruct((4, 4, A, A), F),
            jax.ShapeDtypeStruct((4, 4), F),
        ),
        in_specs=[pl.BlockSpec(memory_space=pltpu.SMEM)] + [pl.BlockSpec(memory_space=pl.ANY)] * 4,
        out_specs=[pl.BlockSpec(memory_space=pltpu.VMEM)] * 3,
        scratch_shapes=[
            tiles(4, 4, 4), tiles(4, 4, 4),
            factor, factor, factor, factor,
            pltpu.VMEM((8, 4, A, A), F),
            pltpu.VMEM((16, C * A, A), F),
            tiles(Q, 64),
            tiles(Q, 4, 8),
            tiles(Q, 3, 8),
            pltpu.VMEM((Q, 8, C, A, A), F),
            tiles(4, 2, 8), tiles(4, 2, 8),
            tiles(Q, 3, 4, 2),
            tiles(Q, 3, 4, 2),
            tiles(Q, 3, 2),
            tiles(Q, 3, 2),
            pltpu.VMEM((5, 8, A), F),
            pltpu.VMEM((10, 8, A), F),
            dma((5,)),
            dma((Q, 2, 12)), dma((Q, 2, 12)),
            dma((Q, 4)), dma((Q, 4)),
            dma((Q, 3)), dma((Q, 3)),
            dma((Q, 10)), dma((Q, 10)),
            dma((Q, 3)), dma((Q, 3)), dma((Q, 3)), dma((Q, 3)),
            dma((Q, 3)), dma((Q, 3)), dma((Q, 3)), dma((Q, 3)),
            dma((10,)), dma((10,)),
        ],
        compiler_params=pltpu.CompilerParams(
            collective_id=1, has_side_effects=True, vmem_limit_bytes=60 * 2**20
        ),
    )(table, coefficients, alpha, beta, denominators)


def in_order(key, fields, targets):
    k = key.shape[1]
    at = jnp.arange(k, dtype=jnp.int32)
    before = (key[:, :, None] > key[:, None, :]) | (
        (key[:, :, None] == key[:, None, :]) & (at[:, None] > at[None, :])
    )
    rank = jnp.sum(before.astype(jnp.int32), axis=2)
    onehot = (rank[:, None, :] == at[None, :, None]).astype(jnp.int32)
    full = jnp.concatenate([fields, key[:, :, None]], axis=2)
    ordered = jnp.sum(onehot[:, :, :, None] * full[:, None, :, :], axis=2)
    key = ordered[:, :, 6]
    keep = (key == jnp.concatenate([jnp.full_like(key[:, :1], -1), key[:, :-1]], axis=1)).astype(jnp.int32)
    ordered = jnp.concatenate([ordered[:, :, :6], keep[:, :, None], keep[:, :, None]], axis=2)
    values = jnp.arange(targets, dtype=jnp.int32)
    last = jnp.sum((key[:, :, None] <= values).astype(jnp.int32), axis=1) - 1
    some = jnp.sum((key[:, :, None] == values).astype(jnp.int32), axis=1) > 0
    return ordered, jnp.maximum(last, 0), some.astype(jnp.int32)


def per_device(coefficients, send_tile, slot_external, slot_pairs, factor_alpha, factor_beta, denominators):
    own = jnp.concatenate(
        [send_tile, slot_external, slot_pairs[0].T, jnp.zeros((3, 128), jnp.int32)], axis=0
    )
    planes, rings = exchange_tables(own)
    x, z, y, c = place()
    pick = lax.dynamic_index_in_dim

    tile_0 = pick(planes[0, :, 0].reshape(16, 16, 8), x * 4 + z, 1, False).T
    tile_1 = pick(planes[1, :, 0].reshape(16, 4, 16, 2), z * 4 + y, 2, False).reshape(16, 8).T
    mine_0 = pick(rings[0].reshape(8, 8, 16, 8), y * 2 + c, 3, False)
    mine_1 = pick(pick(rings[1].reshape(8, 8, 4, 4, 4, 2), x, 2, False), c, 4, False)
    mine_1 = mine_1.swapaxes(2, 3).reshape(8, 8, 16)
    tile = jnp.stack([tile_0, tile_1])
    mine = jnp.stack([mine_0, mine_1])
    external = mine[:, :, 1]
    pairs = mine[:, :, 2:5].transpose(0, 1, 3, 2)
    owner = jnp.arange(16, dtype=jnp.int32)
    receiver = jnp.arange(8, dtype=jnp.int32)

    def fields(index, width, count, value, pairs):
        spread = lambda a: jnp.broadcast_to(a, (2 * count, len(index)))[:, :, None]
        value = value.reshape(2 * count, len(index), 1)
        return jnp.concatenate(
            [spread(index // width), spread(index % width), value, pairs.reshape(2 * count, len(index), 3)],
            axis=2,
        )

    fields_f = fields(owner, 4, 8, tile, pairs)
    fields_b = fields(receiver, 2, 16, external.swapaxes(1, 2), pairs.swapaxes(1, 2))
    parts = [
        *in_order(external.reshape(16, 16), fields_f, 8),
        *in_order(tile.swapaxes(1, 2).reshape(32, 8), fields_b, 4),
    ]
    table = jnp.concatenate([parts[i].reshape(-1) for i in (0, 3, 1, 2, 4, 5)])
    amplitudes, dressing, gram = run_main(table, coefficients, factor_alpha, factor_beta, denominators)
    return amplitudes, dressing, gram


def solution(mesh):
    return jax.shard_map(
        per_device,
        mesh=mesh,
        in_specs=(
            P("dev", None, None, None),
            P("dev", None),
            P("dev", None),
            P("dev", None, None),
            P(),
            P(),
            P("dev", None, None, None),
        ),
        out_specs=(P("dev", None, None, None), P("dev", None, None, None), P()),
        check_vma=False,
    )
```
